32 devices in a mesh: grp: 2 (over x), seq: 4 (over y, core), res: 4 (over z).
Axes of the slice: x: 2, y: 2, z: 4, core: 2. Of those that a mesh axis runs over, the one named last changes fastest.
Arguments:
- alignment_features: bfloat16 [256, 256, 256], P(('grp', 'seq'), 'res'), parts along dimension 0, may hold values from -6 to 6
- scaling_coefficients: float32 [256], replicated, may hold values from 0.1 to 1.9
- first_projector: bfloat16 [256, 32], replicated, may hold values from -0.375 to 0.375
- second_projector: bfloat16 [256, 32], replicated, may hold values from -0.375 to 0.375
- final_projector: float32 [1024, 128], replicated, may hold values from -5 to 5
- final_offset: float32 [128], replicated, may hold values from -3 to 3
Outputs:
- pair: float32 [512, 256, 128], P(('grp', 'res'), 'seq'), parts along dimension 0
The draws below stay inside these ranges and needn't reach their ends.
There are 2 independent parts, one for each index of `grp`. The reference program is written for one: setup_inputs(seed, part) draws one part's arguments, and reference() takes and returns one part's arrays. A program takes and returns all parts, laid end to end along the dimension named above; an argument that names none is the same for every part. Nothing has to cross between parts.
All inputs are finite; a program needn't handle non-finite values.
Results may differ from the reference program's by a relative error of at most 0.0053.
Values may be sent and summed in bfloat16 or wider, within the bound.
A program may use at most 64 MiB of HBM per device.

```python
import jax
import jax.numpy as jnp
from jax import lax

ALIGN_FEAT_WIDTH = 256
PROJ_WIDTH = 32
CZ = 128
ALIGNED_TOTAL = 128
AMINO_TOTAL = 256


def levels(stream_key, shape, split, low, high):
    level, own = 1.0, jax.random.fold_in(stream_key, 6)
    for position, blocks in split:
        steps = jnp.exp(jax.random.uniform(jax.random.fold_in(own, position), (blocks,), jnp.float32, low / len(split), high / len(split)))
        level = level * jnp.repeat(steps, shape[position] // blocks).reshape([-1 if axis == position else 1 for axis in range(len(shape))])
    return level


def centred(key, extent, width, reach, shards=(), dtype=jnp.bfloat16):
    loudness = levels(key, extent, shards, -0.22, 0.18) if shards else 1.0
    drawn = jax.random.normal(key, extent, jnp.float32) * width * loudness
    return jnp.minimum(jnp.maximum(drawn, -reach), reach).astype(dtype)


def setup_inputs(seed: int = 0, part: int = 0) -> dict:
    streams_of = jax.random.split(jax.random.key(seed), 7)
    part_splits = jax.random.split(jax.random.fold_in(streams_of[6], part), 7)
    return {
        "alignment_features": centred(part_splits[0], (ALIGNED_TOTAL, AMINO_TOTAL, ALIGN_FEAT_WIDTH), 1.0, 6.0, ((0, 4), (1, 4))),
        "scaling_coefficients": jnp.clip(1.0 + 0.18 * jax.random.normal(streams_of[1], (ALIGN_FEAT_WIDTH,), jnp.float32), 0.1, 1.9),
        "first_projector": centred(streams_of[2], (ALIGN_FEAT_WIDTH, PROJ_WIDTH), ALIGN_FEAT_WIDTH ** -0.5, 0.375),
        "second_projector": centred(streams_of[3], (ALIGN_FEAT_WIDTH, PROJ_WIDTH), ALIGN_FEAT_WIDTH ** -0.5, 0.375),
        "final_projector": centred(streams_of[4], (PROJ_WIDTH * PROJ_WIDTH, CZ), (0.03 * ALIGNED_TOTAL ** 0.5), 5.0, (), jnp.float32),
        "final_offset": centred(streams_of[5], (CZ,), 0.5, 3.0, (), jnp.float32),
    }


def standardize_rows(values, gain):
    wide = values.astype(jnp.float32)
    center = wide - lax.optimization_barrier(jnp.mean(wide, axis=-1, keepdims=True))
    spread = lax.optimization_barrier(jnp.mean(center * center, axis=-1, keepdims=True))
    return (center * lax.rsqrt(spread + 1e-05) * gain).astype(jnp.bfloat16)

def reference(alignment_features, scaling_coefficients, first_projector, second_projector, final_projector, final_offset):
    standardized_alignment = standardize_rows(alignment_features, scaling_coefficients).reshape(-1, ALIGN_FEAT_WIDTH)
    first_factor = jnp.dot(standardized_alignment, first_projector, preferred_element_type=jnp.float32).astype(jnp.bfloat16)
    second_factor = jnp.dot(standardized_alignment, second_projector, preferred_element_type=jnp.float32).astype(jnp.bfloat16)
    first_factor = first_factor.reshape(ALIGNED_TOTAL, AMINO_TOTAL, PROJ_WIDTH).astype(jnp.float32)
    second_factor = second_factor.reshape(ALIGNED_TOTAL, AMINO_TOTAL, PROJ_WIDTH).astype(jnp.float32)

    def row_block(start):
        block = lax.dynamic_slice_in_dim(first_factor, start, 4, 1)
        outer = jnp.einsum('sic,sje->ijce', block, second_factor, precision=lax.Precision.HIGHEST) * (1.0 / ALIGNED_TOTAL)
        outer = outer.reshape(4 * AMINO_TOTAL, PROJ_WIDTH * PROJ_WIDTH)
        result = jnp.dot(outer, final_projector, precision=lax.Precision.HIGHEST, preferred_element_type=jnp.float32)
        return result.reshape(4, AMINO_TOTAL, CZ) + final_offset
    starts = (jnp.arange(AMINO_TOTAL // 4) * 4).astype(jnp.int32)
    return lax.map(row_block, starts).reshape(AMINO_TOTAL, AMINO_TOTAL, CZ)
```

```python
import functools

import jax
import jax.numpy as jnp
from jax import lax
from jax.experimental import pallas as pl
from jax.experimental.pallas import tpu as pltpu
from jax.sharding import PartitionSpec as P

F32 = jnp.float32
BF16 = jnp.bfloat16
LANES = 128


def kernel(
    dims,
    x_ref,
    gain_ref,
    p1_ref,
    p2_ref,
    w_ref,
    off_ref,
    out_ref,
    normed,
    stacked,
    spread_proj,
    left_all,
    right_own,
    right_all,
    left_t,
    left_mat,
    right_mat,
    outer_mat,
    w_mat,
    left_send,
    left_recv,
    right_send,
    right_recv,
):
    n_seq, n_res, seqs, rows, cols, width, cz, chunk = dims
    per = LANES // width
    blocks = rows // per
    q = n_seq // n_res
    own = blocks // q
    feats = x_ref.shape[1]
    total = n_seq * seqs
    chunks = own // chunk
    half = LANES // 2
    s = lax.axis_index("seq")
    r = lax.axis_index("res")
    home = s // q

    barrier = pltpu.get_barrier_semaphore()
    for d in range(1, n_seq):
        pl.semaphore_signal(barrier, inc=1, device_id={"seq": lax.rem(s + d, n_seq)})
    for t in range(n_seq):
        @pl.when(jnp.logical_or(home != r, t != s))
        def _(t=t):
            pl.semaphore_signal(barrier, inc=1, device_id={"seq": t, "res": home})

    step = 4 * rows

    def norm_rows(i, carry):
        at = pl.ds(pl.multiple_of(i * step, step), step)
        wide = x_ref[at, :].astype(F32)
        center = wide - jnp.mean(wide, axis=-1, keepdims=True)
        spread = jnp.mean(center * center, axis=-1, keepdims=True)
        value = center * lax.rsqrt(spread + 1e-05) * gain_ref[...]
        normed[0, at, :] = value[:, :LANES]
        normed[1, at, :] = value[:, LANES:]
        return carry

    lax.fori_loop(0, seqs * rows // step, norm_rows, 0)

    tile_row = lax.broadcasted_iota(jnp.int32, (width, LANES), 0)
    tile_lane = lax.broadcasted_iota(jnp.int32, (width, LANES), 1)
    tiler = jnp.where(tile_lane % width == tile_row, 1.0, 0.0).astype(BF16)
    wide1 = jnp.dot(p1_ref[...], tiler, preferred_element_type=F32)
    wide2 = jnp.dot(p2_ref[...], tiler, preferred_element_type=F32)
    lane = lax.broadcasted_iota(jnp.int32, (feats, LANES), 1) // width
    for k in range(per):
        at = slice(k * feats, (k + 1) * feats)
        spread_proj[at, :LANES] = jnp.where(lane == k, wide1, 0.0).astype(BF16)
        spread_proj[at, LANES:] = jnp.where(lane == k, wide2, 0.0).astype(BF16)
    for g in range(blocks):
        for k in range(per):
            for h in range(feats // LANES):
                stacked[
                    g * seqs : (g + 1) * seqs, k * feats + h * LANES : k * feats + (h + 1) * LANES
                ] = normed[h, pl.ds(per * g + k, seqs, stride=rows), :].astype(BF16)
    both = jnp.dot(stacked[...], spread_proj[...], preferred_element_type=F32).astype(BF16)
    left_all[s] = both[:, :LANES].reshape(blocks, seqs, LANES)
    right_own[...] = both[:, LANES:].reshape(q * chunks, chunk, seqs, LANES)

    same = jnp.where(home == r, 1, 0)
    pl.semaphore_wait(barrier, n_seq - 1 + q * n_res - same)

    def left_copy(d, source):
        return pltpu.make_async_remote_copy(
            src_ref=left_all.at[source],
            dst_ref=left_all.at[source],
            send_sem=left_send.at[d],
            recv_sem=left_recv.at[source],
            device_id={"seq": lax.rem(s + d, n_seq)},
        )

    def right_copy(b, t, c, source):
        return pltpu.make_async_remote_copy(
            src_ref=right_own.at[b * chunks + c],
            dst_ref=right_all.at[c, source],
            send_sem=right_send.at[b * n_res + t, c],
            recv_sem=right_recv.at[source, c],
            device_id={"seq": r * q + b, "res": t},
        )

    def right_local(b, c):
        return pltpu.make_async_copy(
            right_own.at[b * chunks + c], right_all.at[c, s], right_recv.at[s, c]
        )

    for c in range(chunks):
        for b in range(q):
            for t in range(n_res):
                mine = jnp.logical_and(r * q + b == s, t == r)

                @pl.when(jnp.logical_not(mine))
                def _(b=b, t=t, c=c):
                    right_copy(b, t, c, s).start()

                @pl.when(mine)
                def _(b=b, c=c):
                    right_local(b, c).start()

        if c == 0:
            for d in range(1, n_seq):
                left_copy(d, s).start()

    for c in range(width):
        part = w_ref[c * width : (c + 1) * width, :].astype(BF16)
        zero = jnp.zeros((width, cz), BF16)
        w_mat[2 * c * width : (2 * c + 1) * width, :cz] = part
        w_mat[2 * c * width : (2 * c + 1) * width, cz:] = zero
        w_mat[(2 * c + 1) * width : (2 * c + 2) * width, :cz] = zero
        w_mat[(2 * c + 1) * width : (2 * c + 2) * width, cz:] = part

    for d in range(1, n_seq):
        left_copy(d, lax.rem(s + n_seq - d, n_seq)).wait_recv()
    for g in range(blocks):
        block = left_all[:, g].reshape(total, LANES).astype(F32)
        left_t[:, g * LANES : (g + 1) * LANES, :] = (
            block.T.reshape(LANES, total // LANES, LANES).transpose(1, 0, 2)
            if total > LANES
            else block.T[None]
        )
    for c in range(width):
        for h in range(total // LANES):
            left_mat[
                (c // 2) * rows : (c // 2 + 1) * rows,
                (c % 2) * total + h * LANES : (c % 2) * total + (h + 1) * LANES,
            ] = left_t[h, pl.ds(c, rows, stride=width), :].astype(BF16)

    low = lax.broadcasted_iota(jnp.int32, (total, LANES), 1) < half
    scale = 1.0 / total
    for c in range(chunks):
        for t in range(n_seq):
            right_copy(0, 0, c, t).wait_recv()
        for g in range(chunk):
            block = right_all[c, :, g].reshape(total, LANES).astype(F32)
            turned = pltpu.roll(block, half, 1)
            right_mat[:total, :LANES] = jnp.where(low, block, 0.0).astype(BF16)
            right_mat[total:, :LANES] = jnp.where(low, 0.0, turned).astype(BF16)
            right_mat[:total, LANES:] = jnp.where(low, turned, 0.0).astype(BF16)
            right_mat[total:, LANES:] = jnp.where(low, 0.0, block).astype(BF16)
            outer = jnp.dot(left_mat[...], right_mat[...], preferred_element_type=F32).astype(BF16)
            for h in range(2):
                for p in range(width // 2):
                    outer_mat[
                        (2 * g + h) * rows : (2 * g + h + 1) * rows, p * LANES : (p + 1) * LANES
                    ] = outer[p * rows : (p + 1) * rows, h * LANES : (h + 1) * LANES]
        result = jnp.dot(outer_mat[...], w_mat[...], preferred_element_type=F32)
        for p in range(2 * chunk):
            for h in range(2):
                col = (c * chunk * 2 + p) * 2 + h
                out_ref[pl.ds(col, rows, stride=cols), :] = (
                    result[p * rows : (p + 1) * rows, h * cz : (h + 1) * cz] * scale + off_ref[...]
                )

    for d in range(1, n_seq):
        left_copy(d, s).wait_send()
    for c in range(chunks):
        for b in range(q):
            for t in range(n_res):
                mine = jnp.logical_and(r * q + b == s, t == r)

                @pl.when(jnp.logical_not(mine))
                def _(b=b, t=t, c=c):
                    right_copy(b, t, c, s).wait_send()


def local(n_seq, n_res, features, gain, p1, p2, w, offset):
    seqs, rows, feats = features.shape
    width = p1.shape[1]
    cz = w.shape[1]
    cols = rows * n_res // n_seq
    per = LANES // width
    blocks = rows // per
    q = n_seq // n_res
    own = blocks // q
    chunk = 4
    chunks = own // chunk
    total = n_seq * seqs
    dims = (n_seq, n_res, seqs, rows, cols, width, cz, chunk)
    vmem = pl.BlockSpec(memory_space=pltpu.VMEM)
    out = pl.pallas_call(
        functools.partial(kernel, dims),
        out_shape=jax.ShapeDtypeStruct((rows * cols, cz), F32),
        in_specs=[vmem] * 6,
        out_specs=vmem,
        scratch_shapes=[
            pltpu.VMEM((feats // LANES, seqs * rows, LANES), F32),
            pltpu.VMEM((blocks * seqs, per * feats), BF16),
            pltpu.VMEM((per * feats, 2 * LANES), BF16),
            pltpu.VMEM((n_seq, blocks, seqs, LANES), BF16),
            pltpu.VMEM((q * chunks, chunk, seqs, LANES), BF16),
            pltpu.VMEM((chunks, n_seq, chunk, seqs, LANES), BF16),
            pltpu.VMEM((total // LANES, rows * width, LANES), F32),
            pltpu.VMEM((width // 2 * rows, 2 * total), BF16),
            pltpu.VMEM((2 * total, 2 * LANES), BF16),
            pltpu.VMEM((chunk * 2 * rows, width // 2 * LANES), BF16),
            pltpu.VMEM((2 * width * width, 2 * cz), BF16),
            pltpu.SemaphoreType.DMA((n_seq,)),
            pltpu.SemaphoreType.DMA((n_seq,)),
            pltpu.SemaphoreType.DMA((n_seq, chunks)),
            pltpu.SemaphoreType.DMA((n_seq, chunks)),
        ],
        compiler_params=pltpu.CompilerParams(
            collective_id=0, has_side_effects=True, vmem_limit_bytes=48 * 1024 * 1024
        ),
    )(
        features.reshape(seqs * rows, feats),
        gain.reshape(1, feats),
        p1,
        p2,
        w,
        offset.reshape(1, cz),
    )
    return out.reshape(rows, cols, cz)


def solution(mesh):
    return jax.shard_map(
        functools.partial(local, mesh.shape["seq"], mesh.shape["res"]),
        mesh=mesh,
        in_specs=(P(("grp", "seq"), "res", None), P(), P(), P(), P(), P()),
        out_specs=P(("grp", "res"), "seq", None),
        check_vma=False,
    )
```

```python
import functools

import jax
import jax.numpy as jnp
from jax import lax
from jax.experimental import pallas as pl
from jax.experimental.pallas import tpu as pltpu
from jax.sharding import PartitionSpec as P

F32 = jnp.float32
BF16 = jnp.bfloat16
LANES = 128


def kernel(
    dims,
    x_ref,
    gain_ref,
    p1_ref,
    p2_ref,
    w_ref,
    off_ref,
    out_ref,
    x_in,
    gain_in,
    p1_in,
    p2_in,
    w_in,
    off_in,
    normed,
    stacked,
    spread_proj,
    left_all,
    right_own,
    right_all,
    left_t,
    left_mat,
    right_mat,
    outer_mat,
    w_mat,
    left_send,
    left_recv,
    right_send,
    right_recv,
    x_sem,
    in_sem,
):
    n_seq, n_res, seqs, rows, cols, width, cz, chunk = dims
    per = LANES // width
    blocks = rows // per
    q = n_seq // n_res
    own = blocks // q
    feats = x_ref.shape[2]
    total = n_seq * seqs
    chunks = own // chunk
    parts = blocks // chunk
    some = per * chunk
    half = LANES // 2
    s = lax.axis_index("seq")
    r = lax.axis_index("res")
    home = s // q

    def x_copy(k):
        at = (slice(None), slice(k * some, (k + 1) * some))
        return pltpu.make_async_copy(x_ref.at[at], x_in.at[at], x_sem.at[k])

    small = [
        pltpu.make_async_copy(a, b, in_sem.at[n])
        for n, (a, b) in enumerate(
            [
                (p1_ref, p1_in),
                (p2_ref, p2_in),
                (gain_ref, gain_in),
                (off_ref, off_in),
                (w_ref, w_in),
            ]
        )
    ]
    x_copy(0).start()
    for copy in small[:4]:
        copy.start()
    for k in range(1, parts):
        x_copy(k).start()
    small[4].start()

    barrier = pltpu.get_barrier_semaphore()
    for d in range(1, n_seq):
        pl.semaphore_signal(barrier, inc=1, device_id={"seq": lax.rem(s + d, n_seq)})
    for t in range(n_seq):
        @pl.when(jnp.logical_or(home != r, t != s))
        def _(t=t):
            pl.semaphore_signal(barrier, inc=1, device_id={"seq": t, "res": home})

    def left_copy(d, k, source):
        return pltpu.make_async_remote_copy(
            src_ref=left_all.at[k, source],
            dst_ref=left_all.at[k, source],
            send_sem=left_send.at[d, k],
            recv_sem=left_recv.at[source, k],
            device_id={"seq": lax.rem(s + d, n_seq)},
        )

    def left_pass(d, k, source):
        return pltpu.make_async_remote_copy(
            src_ref=left_all.at[k, source],
            dst_ref=left_all.at[k, source],
            send_sem=left_send.at[d + 1, k],
            recv_sem=left_recv.at[source, k],
            device_id={"seq": s + 1 - 2 * lax.rem(s, 2)},
        )

    def right_copy(b, t, c, source):
        return pltpu.make_async_remote_copy(
            src_ref=right_own.at[b * chunks + c],
            dst_ref=right_all.at[c, source],
            send_sem=right_send.at[b * n_res + t, c],
            recv_sem=right_recv.at[source, c],
            device_id={"seq": r * q + b, "res": t},
        )

    def right_local(b, c):
        return pltpu.make_async_copy(
            right_own.at[b * chunks + c], right_all.at[c, s], right_recv.at[s, c]
        )

    def right_start(k):
        b, c = k // chunks, k % chunks
        for t in range(n_res):
            mine = jnp.logical_and(r * q + b == s, t == r)

            @pl.when(jnp.logical_not(mine))
            def _(t=t):
                right_copy(b, t, c, s).start()

            @pl.when(mine)
            def _():
                right_local(b, c).start()

    def right_sent(k):
        b, c = k // chunks, k % chunks
        for t in range(n_res):
            mine = jnp.logical_and(r * q + b == s, t == r)

            @pl.when(jnp.logical_not(mine))
            def _(t=t):
                right_copy(b, t, c, s).wait_send()

    for copy in small[:3]:
        copy.wait()
    tile_row = lax.broadcasted_iota(jnp.int32, (width, LANES), 0)
    tile_lane = lax.broadcasted_iota(jnp.int32, (width, LANES), 1)
    tiler = jnp.where(tile_lane % width == tile_row, 1.0, 0.0).astype(BF16)
    first = (((0,), (0,)), ((), ()))
    wide1 = lax.dot_general(p1_in[...], tiler, first, preferred_element_type=F32)
    wide2 = lax.dot_general(p2_in[...], tiler, first, preferred_element_type=F32)
    lane = lax.broadcasted_iota(jnp.int32, (feats, LANES), 1) // width
    for k in range(per):
        at = slice(k * feats, (k + 1) * feats)
        spread_proj[at, :LANES] = jnp.where(lane == k, wide1, 0.0).astype(BF16)
        spread_proj[at, LANES:] = jnp.where(lane == k, wide2, 0.0).astype(BF16)

    same = jnp.where(home == r, 1, 0)
    step = 8
    gain = gain_in[...]
    ones = jnp.ones((feats, feats), BF16)
    for k in range(parts):
        x_copy(k).wait()
        for n in range(seqs // step):
            block = x_in[n * step : (n + 1) * step, k * some : (k + 1) * some, :]
            wide = block.reshape(step * some, feats).astype(F32)
            rowsum = jnp.dot(block.reshape(step * some, feats), ones, preferred_element_type=F32)
            center = wide - rowsum * (1.0 / feats)
            square = center * center
            high = square.astype(BF16)
            rest = (square - high.astype(F32)).astype(BF16)
            spread = jnp.dot(high, ones, preferred_element_type=F32) + jnp.dot(
                rest, ones, preferred_element_type=F32
            )
            value = center * lax.rsqrt(spread * (1.0 / feats) + 1e-05) * gain
            for h in range(feats // LANES):
                normed[k, h, n * step * some : (n + 1) * step * some, :] = value[
                    :, h * LANES : (h + 1) * LANES
                ]
        for g in range(chunk):
            for j in range(per):
                for h in range(feats // LANES):
                    at = j * feats + h * LANES
                    stacked[k, g * seqs : (g + 1) * seqs, at : at + LANES] = normed[
                        k, h, pl.ds(per * g + j, seqs, stride=some), :
                    ].astype(BF16)
        both = jnp.dot(stacked[k], spread_proj[...], preferred_element_type=F32).astype(BF16)
        left_all[k, s] = both[:, :LANES].reshape(chunk, seqs, LANES)
        right_own[k] = both[:, LANES:].reshape(chunk, seqs, LANES)
        if k == 0:
            pl.semaphore_wait(barrier, n_seq - 1 + q * n_res - same)
        for d in range(2, n_seq, 2):
            left_copy(d, k, s).start()
        left_pass(0, k, s).start()
        if k < 2:
            right_start(k)

    small[3].wait()
    small[4].wait()
    zero = jnp.zeros((width, cz), BF16)
    for c in range(width):
        part = w_in[c * width : (c + 1) * width, :].astype(BF16)
        w_mat[2 * c * width : (2 * c + 1) * width, :cz] = part
        w_mat[2 * c * width : (2 * c + 1) * width, cz:] = zero
        w_mat[(2 * c + 1) * width : (2 * c + 2) * width, :cz] = zero
        w_mat[(2 * c + 1) * width : (2 * c + 2) * width, cz:] = part

    for k in range(parts):
        for d in range(2, n_seq, 2):
            source = lax.rem(s + n_seq - d, n_seq)
            left_copy(d, k, source).wait_recv()
            left_pass(d, k, source).start()
    for k in range(2, parts):
        right_sent(k - 2)
        right_start(k)
    for k in range(parts):
        for d in range(0, n_seq, 2):
            left_copy(0, k, lax.rem(s + 1 - 2 * lax.rem(s, 2) + n_seq - d, n_seq)).wait_recv()
        for g in range(chunk):
            block = left_all[k, :, g].reshape(total, LANES).astype(F32).T
            for h in range(total // LANES):
                at = (k * chunk + g) * LANES
                left_t[h, at : at + LANES, :] = block[:, h * LANES : (h + 1) * LANES]
    for c in range(width):
        for h in range(total // LANES):
            left_mat[
                (c // 2) * rows : (c // 2 + 1) * rows,
                (c % 2) * total + h * LANES : (c % 2) * total + (h + 1) * LANES,
            ] = left_t[h, pl.ds(c, rows, stride=width), :].astype(BF16)
    low = lax.broadcasted_iota(jnp.int32, (total, LANES), 1) < half
    scale = 1.0 / total
    for c in range(chunks):
        for t in range(n_seq):
            right_copy(0, 0, c, t).wait_recv()
        for g in range(chunk):
            block = right_all[c, :, g].reshape(total, LANES).astype(F32)
            turned = pltpu.roll(block, half, 1)
            right_mat[:total, :LANES] = jnp.where(low, block, 0.0).astype(BF16)
            right_mat[total:, :LANES] = jnp.where(low, 0.0, turned).astype(BF16)
            right_mat[:total, LANES:] = jnp.where(low, turned, 0.0).astype(BF16)
            right_mat[total:, LANES:] = jnp.where(low, 0.0, block).astype(BF16)
            outer = jnp.dot(left_mat[...], right_mat[...], preferred_element_type=F32).astype(BF16)
            for h in range(2):
                for p in range(width // 2):
                    outer_mat[
                        (2 * g + h) * rows : (2 * g + h + 1) * rows, p * LANES : (p + 1) * LANES
                    ] = outer[p * rows : (p + 1) * rows, h * LANES : (h + 1) * LANES]
        result = jnp.dot(outer_mat[...], w_mat[...], preferred_element_type=F32)
        for p in range(2 * chunk):
            for h in range(2):
                col = (c * chunk * 2 + p) * 2 + h
                out_ref[pl.ds(col, rows, stride=cols), :] = (
                    result[p * rows : (p + 1) * rows, h * cz : (h + 1) * cz] * scale + off_in[...]
                )

    for k in range(parts):
        for d in range(2, n_seq, 2):
            left_copy(d, k, s).wait_send()
        for d in range(0, n_seq, 2):
            left_pass(d, k, s).wait_send()
    for k in range(max(parts - 2, 0), parts):
        right_sent(k)


def local(n_seq, n_res, features, gain, p1, p2, w, offset):
    seqs, rows, feats = features.shape
    width = p1.shape[1]
    cz = w.shape[1]
    cols = rows * n_res // n_seq
    per = LANES // width
    blocks = rows // per
    q = n_seq // n_res
    own = blocks // q
    chunk = 4
    chunks = own // chunk
    total = n_seq * seqs
    dims = (n_seq, n_res, seqs, rows, cols, width, cz, chunk)
    parts = blocks // chunk
    hbm = pl.BlockSpec(memory_space=pltpu.HBM)
    out = pl.pallas_call(
        functools.partial(kernel, dims),
        out_shape=jax.ShapeDtypeStruct((rows * cols, cz), F32),
        in_specs=[hbm] * 6,
        out_specs=pl.BlockSpec(memory_space=pltpu.VMEM),
        scratch_shapes=[
            pltpu.VMEM((seqs, rows, feats), BF16),
            pltpu.VMEM((1, feats), F32),
            pltpu.VMEM((width, feats), BF16),
            pltpu.VMEM((width, feats), BF16),
            pltpu.VMEM(w.shape, F32),
            pltpu.VMEM((1, cz), F32),
            pltpu.VMEM((parts, feats // LANES, seqs * per * chunk, LANES), F32),
            pltpu.VMEM((parts, chunk * seqs, per * feats), BF16),
            pltpu.VMEM((per * feats, 2 * LANES), BF16),
            pltpu.VMEM((parts, n_seq, chunk, seqs, LANES), BF16),
            pltpu.VMEM((parts, chunk, seqs, LANES), BF16),
            pltpu.VMEM((chunks, n_seq, chunk, seqs, LANES), BF16),
            pltpu.VMEM((total // LANES, rows * width, LANES), F32),
            pltpu.VMEM((width // 2 * rows, 2 * total), BF16),
            pltpu.VMEM((2 * total, 2 * LANES), BF16),
            pltpu.VMEM((chunk * 2 * rows, width // 2 * LANES), BF16),
            pltpu.VMEM((2 * width * width, 2 * cz), BF16),
            pltpu.SemaphoreType.DMA((n_seq, parts)),
            pltpu.SemaphoreType.DMA((n_seq, parts)),
            pltpu.SemaphoreType.DMA((n_seq, chunks)),
            pltpu.SemaphoreType.DMA((n_seq, chunks)),
            pltpu.SemaphoreType.DMA((parts,)),
            pltpu.SemaphoreType.DMA((5,)),
        ],
        compiler_params=pltpu.CompilerParams(
            collective_id=0, has_side_effects=True, vmem_limit_bytes=62 * 1024 * 1024
        ),
    )(features, gain.reshape(1, feats), p1.T, p2.T, w, offset.reshape(1, cz))
    return out.reshape(rows, cols, cz)


def solution(mesh):
    return jax.shard_map(
        functools.partial(local, mesh.shape["seq"], mesh.shape["res"]),
        mesh=mesh,
        in_specs=(P(("grp", "seq"), "res", None), P(), P(), P(), P(), P()),
        out_specs=P(("grp", "res"), "seq", None),
        check_vma=False,
    )
```

```python
import functools

import jax
import jax.numpy as jnp
from jax import lax
from jax.experimental import pallas as pl
from jax.experimental.pallas import tpu as pltpu
from jax.sharding import PartitionSpec as P

F32 = jnp.float32
BF16 = jnp.bfloat16
LANES = 128


def kernel(
    dims,
    x_ref,
    gain_ref,
    p1_ref,
    p2_ref,
    left_mat,
    right_all,
    x_in,
    gain_in,
    p1_in,
    p2_in,
    normed,
    stacked,
    spread_proj,
    left_all,
    right_own,
    left_t,
    left_send,
    left_recv,
    right_send,
    right_recv,
    x_sem,
    in_sem,
):
    n_seq, n_res, seqs, rows, cols, width, cz, chunk = dims
    per = LANES // width
    blocks = rows // per
    q = n_seq // n_res
    own = blocks // q
    feats = x_ref.shape[2]
    total = n_seq * seqs
    chunks = own // chunk
    parts = blocks // chunk
    some = per * chunk
    half = LANES // 2
    s = lax.axis_index("seq")
    r = lax.axis_index("res")
    home = s // q

    def x_copy(k):
        at = (slice(None), slice(k * some, (k + 1) * some))
        return pltpu.make_async_copy(x_ref.at[at], x_in.at[at], x_sem.at[k])

    small = [
        pltpu.make_async_copy(a, b, in_sem.at[n])
        for n, (a, b) in enumerate(
            [
                (p1_ref, p1_in),
                (p2_ref, p2_in),
                (gain_ref, gain_in),
            ]
        )
    ]
    x_copy(0).start()
    for copy in small:
        copy.start()
    for k in range(1, parts):
        x_copy(k).start()

    barrier = pltpu.get_barrier_semaphore()
    for d in range(1, n_seq):
        pl.semaphore_signal(barrier, inc=1, device_id={"seq": lax.rem(s + d, n_seq)})
    for t in range(n_seq):
        @pl.when(jnp.logical_or(home != r, t != s))
        def _(t=t):
            pl.semaphore_signal(barrier, inc=1, device_id={"seq": t, "res": home})

    def left_copy(d, k, source):
        return pltpu.make_async_remote_copy(
            src_ref=left_all.at[k, source],
            dst_ref=left_all.at[k, source],
            send_sem=left_send.at[d, k],
            recv_sem=left_recv.at[source, k],
            device_id={"seq": lax.rem(s + d, n_seq)},
        )

    def left_pass(d, k, source):
        return pltpu.make_async_remote_copy(
            src_ref=left_all.at[k, source],
            dst_ref=left_all.at[k, source],
            send_sem=left_send.at[d + 1, k],
            recv_sem=left_recv.at[source, k],
            device_id={"seq": s + 1 - 2 * lax.rem(s, 2)},
        )

    def right_copy(b, t, c, source):
        return pltpu.make_async_remote_copy(
            src_ref=right_own.at[b * chunks + c],
            dst_ref=right_all.at[c, source],
            send_sem=right_send.at[b * n_res + t, c],
            recv_sem=right_recv.at[source, c],
            device_id={"seq": r * q + b, "res": t},
        )

    def right_local(b, c):
        return pltpu.make_async_copy(
            right_own.at[b * chunks + c], right_all.at[c, s], right_recv.at[s, c]
        )

    def right_start(k):
        b, c = k // chunks, k % chunks
        for t in range(n_res):
            mine = jnp.logical_and(r * q + b == s, t == r)

            @pl.when(jnp.logical_not(mine))
            def _(t=t):
                right_copy(b, t, c, s).start()

            @pl.when(mine)
            def _():
                right_local(b, c).start()

    def right_sent(k):
        b, c = k // chunks, k % chunks
        for t in range(n_res):
            mine = jnp.logical_and(r * q + b == s, t == r)

            @pl.when(jnp.logical_not(mine))
            def _(t=t):
                right_copy(b, t, c, s).wait_send()

    for copy in small:
        copy.wait()
    tile_row = lax.broadcasted_iota(jnp.int32, (width, LANES), 0)
    tile_lane = lax.broadcasted_iota(jnp.int32, (width, LANES), 1)
    tiler = jnp.where(tile_lane % width == tile_row, 1.0, 0.0).astype(BF16)
    first = (((0,), (0,)), ((), ()))
    wide1 = lax.dot_general(p1_in[...], tiler, first, preferred_element_type=F32)
    wide2 = lax.dot_general(p2_in[...], tiler, first, preferred_element_type=F32)
    lane = lax.broadcasted_iota(jnp.int32, (feats, LANES), 1) // width
    for k in range(per):
        at = slice(k * feats, (k + 1) * feats)
        spread_proj[at, :LANES] = jnp.where(lane == k, wide1, 0.0).astype(BF16)
        spread_proj[at, LANES:] = jnp.where(lane == k, wide2, 0.0).astype(BF16)

    same = jnp.where(home == r, 1, 0)
    step = 8
    gain = gain_in[...]
    ones = jnp.ones((feats, feats), BF16)
    for k in range(parts):
        x_copy(k).wait()
        for n in range(seqs // step):
            block = x_in[n * step : (n + 1) * step, k * some : (k + 1) * some, :]
            wide = block.reshape(step * some, feats).astype(F32)
            rowsum = jnp.dot(block.reshape(step * some, feats), ones, preferred_element_type=F32)
            center = wide - rowsum * (1.0 / feats)
            square = center * center
            high = square.astype(BF16)
            rest = (square - high.astype(F32)).astype(BF16)
            spread = jnp.dot(high, ones, preferred_element_type=F32) + jnp.dot(
                rest, ones, preferred_element_type=F32
            )
            value = center * lax.rsqrt(spread * (1.0 / feats) + 1e-05) * gain
            for h in range(feats // LANES):
                normed[k, h, n * step * some : (n + 1) * step * some, :] = value[
                    :, h * LANES : (h + 1) * LANES
                ]
        for g in range(chunk):
            for j in range(per):
                for h in range(feats // LANES):
                    at = j * feats + h * LANES
                    stacked[k, g * seqs : (g + 1) * seqs, at : at + LANES] = normed[
                        k, h, pl.ds(per * g + j, seqs, stride=some), :
                    ].astype(BF16)
        both = jnp.dot(stacked[k], spread_proj[...], preferred_element_type=F32).astype(BF16)
        left_all[k, s] = both[:, :LANES].reshape(chunk, seqs, LANES)
        right_own[k] = both[:, LANES:].reshape(chunk, seqs, LANES)
        if k == 0:
            pl.semaphore_wait(barrier, n_seq - 1 + q * n_res - same)
        for d in range(2, n_seq, 2):
            left_copy(d, k, s).start()
        left_pass(0, k, s).start()
        if k < 2:
            right_start(k)

    for k in range(parts):
        for d in range(2, n_seq, 2):
            source = lax.rem(s + n_seq - d, n_seq)
            left_copy(d, k, source).wait_recv()
            left_pass(d, k, source).start()
    for k in range(2, parts):
        right_sent(k - 2)
        right_start(k)
    for k in range(parts):
        for d in range(0, n_seq, 2):
            left_copy(0, k, lax.rem(s + 1 - 2 * lax.rem(s, 2) + n_seq - d, n_seq)).wait_recv()
        for g in range(chunk):
            block = left_all[k, :, g].reshape(total, LANES).astype(F32).T
            for h in range(total // LANES):
                at = (k * chunk + g) * LANES
                left_t[h, at : at + LANES, :] = block[:, h * LANES : (h + 1) * LANES]
    for c in range(width):
        for h in range(total // LANES):
            left_mat[
                (c // 2) * rows : (c // 2 + 1) * rows,
                (c % 2) * total + h * LANES : (c % 2) * total + (h + 1) * LANES,
            ] = left_t[h, pl.ds(c, rows, stride=width), :].astype(BF16)
    for c in range(chunks):
        for t in range(n_seq):
            right_copy(0, 0, c, t).wait_recv()
    for k in range(parts):
        for d in range(2, n_seq, 2):
            left_copy(d, k, s).wait_send()
        for d in range(0, n_seq, 2):
            left_pass(d, k, s).wait_send()
    for k in range(max(parts - 2, 0), parts):
        right_sent(k)


def pair_kernel(
    dims,
    left_hbm,
    right_hbm,
    w_hbm,
    off_hbm,
    out_ref,
    left_mat,
    right_all,
    w_ref,
    off_ref,
    right_mat,
    outer_mat,
    w_mat,
    out_buf,
    sem,
    in_sem,
):
    n_seq, n_res, seqs, rows, cols, width, cz, chunk = dims
    chunks = right_all.shape[0]
    total = n_seq * seqs
    half = LANES // 2
    some = cols // chunks
    arrive = [
        pltpu.make_async_copy(a, b, in_sem.at[n])
        for n, (a, b) in enumerate(
            [(w_hbm, w_ref), (left_hbm, left_mat), (right_hbm, right_all), (off_hbm, off_ref)]
        )
    ]
    for copy in arrive:
        copy.start()
    arrive[0].wait()

    def send(c):
        return pltpu.make_async_copy(
            out_buf.at[c].reshape(rows, some, cz),
            out_ref.at[:, c * some : (c + 1) * some],
            sem.at[c],
        )

    zero = jnp.zeros((width, cz), BF16)
    for c in range(width):
        part = w_ref[c * width : (c + 1) * width, :].astype(BF16)
        w_mat[2 * c * width : (2 * c + 1) * width, :cz] = part
        w_mat[2 * c * width : (2 * c + 1) * width, cz:] = zero
        w_mat[(2 * c + 1) * width : (2 * c + 2) * width, :cz] = zero
        w_mat[(2 * c + 1) * width : (2 * c + 2) * width, cz:] = part

    for copy in arrive[1:]:
        copy.wait()
    low = lax.broadcasted_iota(jnp.int32, (total, LANES), 1) < half
    scale = 1.0 / total
    for c in range(chunks):
        for g in range(chunk):
            block = right_all[c, :, g].reshape(total, LANES).astype(F32)
            turned = pltpu.roll(block, half, 1)
            right_mat[:total, :LANES] = jnp.where(low, block, 0.0).astype(BF16)
            right_mat[total:, :LANES] = jnp.where(low, 0.0, turned).astype(BF16)
            right_mat[:total, LANES:] = jnp.where(low, turned, 0.0).astype(BF16)
            right_mat[total:, LANES:] = jnp.where(low, 0.0, block).astype(BF16)
            outer = jnp.dot(left_mat[...], right_mat[...], preferred_element_type=F32).astype(BF16)
            for h in range(2):
                for p in range(width // 2):
                    outer_mat[
                        (2 * g + h) * rows : (2 * g + h + 1) * rows, p * LANES : (p + 1) * LANES
                    ] = outer[p * rows : (p + 1) * rows, h * LANES : (h + 1) * LANES]
        result = jnp.dot(outer_mat[...], w_mat[...], preferred_element_type=F32)
        for p in range(2 * chunk):
            for h in range(2):
                col = p * 2 + h
                out_buf[c, pl.ds(col, rows, stride=some), :] = (
                    result[p * rows : (p + 1) * rows, h * cz : (h + 1) * cz] * scale + off_ref[...]
                )
        send(c).start()
    for c in range(chunks):
        send(c).wait()


def local(n_seq, n_res, features, gain, p1, p2, w, offset):
    seqs, rows, feats = features.shape
    width = p1.shape[1]
    cz = w.shape[1]
    cols = rows * n_res // n_seq
    per = LANES // width
    blocks = rows // per
    q = n_seq // n_res
    own = blocks // q
    chunk = 4
    chunks = own // chunk
    total = n_seq * seqs
    dims = (n_seq, n_res, seqs, rows, cols, width, cz, chunk)
    parts = blocks // chunk
    hbm = pl.BlockSpec(memory_space=pltpu.HBM)
    vmem = pl.BlockSpec(memory_space=pltpu.VMEM)
    left, right = pl.pallas_call(
        functools.partial(kernel, dims),
        out_shape=[
            jax.ShapeDtypeStruct((width // 2 * rows, 2 * total), BF16),
            jax.ShapeDtypeStruct((chunks, n_seq, chunk, seqs, LANES), BF16),
        ],
        in_specs=[hbm] * 4,
        out_specs=[vmem] * 2,
        scratch_shapes=[
            pltpu.VMEM((seqs, rows, feats), BF16),
            pltpu.VMEM((1, feats), F32),
            pltpu.VMEM((width, feats), BF16),
            pltpu.VMEM((width, feats), BF16),
            pltpu.VMEM((parts, feats // LANES, seqs * per * chunk, LANES), F32),
            pltpu.VMEM((parts, chunk * seqs, per * feats), BF16),
            pltpu.VMEM((per * feats, 2 * LANES), BF16),
            pltpu.VMEM((parts, n_seq, chunk, seqs, LANES), BF16),
            pltpu.VMEM((parts, chunk, seqs, LANES), BF16),
            pltpu.VMEM((total // LANES, rows * width, LANES), F32),
            pltpu.SemaphoreType.DMA((n_seq, parts)),
            pltpu.SemaphoreType.DMA((n_seq, parts)),
            pltpu.SemaphoreType.DMA((n_seq, chunks)),
            pltpu.SemaphoreType.DMA((n_seq, chunks)),
            pltpu.SemaphoreType.DMA((parts,)),
            pltpu.SemaphoreType.DMA((3,)),
        ],
        compiler_params=pltpu.CompilerParams(
            collective_id=0, has_side_effects=True, vmem_limit_bytes=62 * 1024 * 1024
        ),
    )(features, gain.reshape(1, feats), p1.T, p2.T)
    return pl.pallas_call(
        functools.partial(pair_kernel, dims),
        out_shape=jax.ShapeDtypeStruct((rows, cols, cz), F32),
        in_specs=[hbm] * 4,
        out_specs=hbm,
        scratch_shapes=[
            pltpu.VMEM(left.shape, BF16),
            pltpu.VMEM(right.shape, BF16),
            pltpu.VMEM(w.shape, F32),
            pltpu.VMEM((1, cz), F32),
            pltpu.VMEM((2 * total, 2 * LANES), BF16),
            pltpu.VMEM((chunk * 2 * rows, width // 2 * LANES), BF16),
            pltpu.VMEM((2 * width * width, 2 * cz), BF16),
            pltpu.VMEM((chunks, rows * (cols // chunks), cz), F32),
            pltpu.SemaphoreType.DMA((chunks,)),
            pltpu.SemaphoreType.DMA((4,)),
        ],
        compiler_params=pltpu.CompilerParams(vmem_limit_bytes=62 * 1024 * 1024),
    )(left, right, w, offset.reshape(1, cz))


def solution(mesh):
    return jax.shard_map(
        functools.partial(local, mesh.shape["seq"], mesh.shape["res"]),
        mesh=mesh,
        in_specs=(P(("grp", "seq"), "res", None), P(), P(), P(), P(), P()),
        out_specs=P(("grp", "res"), "seq", None),
        check_vma=False,
    )
```

```python
import functools

import jax
import jax.numpy as jnp
from jax import lax
from jax.experimental import pallas as pl
from jax.experimental.pallas import tpu as pltpu
from jax.sharding import PartitionSpec as P

F32 = jnp.float32
BF16 = jnp.bfloat16
LANES = 128


def kernel(
    dims,
    x_ref,
    gain_ref,
    p1_ref,
    p2_ref,
    left_mat,
    right_all,
    x_in,
    gain_in,
    p1_in,
    p2_in,
    normed,
    stacked,
    spread_proj,
    left_all,
    right_own,
    left_t,
    left_send,
    left_recv,
    right_send,
    right_recv,
    x_sem,
    in_sem,
):
    n_seq, n_res, seqs, rows, cols, width, cz, chunk = dims
    per = LANES // width
    blocks = rows // per
    q = n_seq // n_res
    own = blocks // q
    feats = x_ref.shape[2]
    total = n_seq * seqs
    chunks = own // chunk
    parts = blocks // chunk
    some = per * chunk
    half = LANES // 2
    s = lax.axis_index("seq")
    r = lax.axis_index("res")
    home = s // q

    def x_copy(k):
        at = (slice(None), slice(k * some, (k + 1) * some))
        return pltpu.make_async_copy(x_ref.at[at], x_in.at[at], x_sem.at[k])

    small = [
        pltpu.make_async_copy(a, b, in_sem.at[n])
        for n, (a, b) in enumerate(
            [
                (p1_ref, p1_in),
                (p2_ref, p2_in),
                (gain_ref, gain_in),
            ]
        )
    ]
    x_copy(0).start()
    for copy in small:
        copy.start()
    for k in range(1, parts):
        x_copy(k).start()

    barrier = pltpu.get_barrier_semaphore()
    for d in range(1, n_seq):
        pl.semaphore_signal(barrier, inc=1, device_id={"seq": lax.rem(s + d, n_seq)})
    for t in range(n_seq):
        @pl.when(jnp.logical_or(home != r, t != s))
        def _(t=t):
            pl.semaphore_signal(barrier, inc=1, device_id={"seq": t, "res": home})

    def left_copy(d, k, source):
        return pltpu.make_async_remote_copy(
            src_ref=left_all.at[k, source],
            dst_ref=left_all.at[k, source],
            send_sem=left_send.at[d, k],
            recv_sem=left_recv.at[source, k],
            device_id={"seq": lax.rem(s + d, n_seq)},
        )

    def left_pass(d, k, source):
        return pltpu.make_async_remote_copy(
            src_ref=left_all.at[k, source],
            dst_ref=left_all.at[k, source],
            send_sem=left_send.at[d + 1, k],
            recv_sem=left_recv.at[source, k],
            device_id={"seq": s + 1 - 2 * lax.rem(s, 2)},
        )

    def right_copy(b, t, c, source):
        return pltpu.make_async_remote_copy(
            src_ref=right_own.at[b * chunks + c],
            dst_ref=right_all.at[c, source],
            send_sem=right_send.at[b * n_res + t, c],
            recv_sem=right_recv.at[source, c],
            device_id={"seq": r * q + b, "res": t},
        )

    def right_local(b, c):
        return pltpu.make_async_copy(
            right_own.at[b * chunks + c], right_all.at[c, s], right_recv.at[s, c]
        )

    def right_start(k):
        b, c = k // chunks, k % chunks
        for t in range(n_res):
            mine = jnp.logical_and(r * q + b == s, t == r)

            @pl.when(jnp.logical_not(mine))
            def _(t=t):
                right_copy(b, t, c, s).start()

            @pl.when(mine)
            def _():
                right_local(b, c).start()

    def right_sent(k):
        b, c = k // chunks, k % chunks
        for t in range(n_res):
            mine = jnp.logical_and(r * q + b == s, t == r)

            @pl.when(jnp.logical_not(mine))
            def _(t=t):
                right_copy(b, t, c, s).wait_send()

    for copy in small:
        copy.wait()
    tile_row = lax.broadcasted_iota(jnp.int32, (width, LANES), 0)
    tile_lane = lax.broadcasted_iota(jnp.int32, (width, LANES), 1)
    tiler = jnp.where(tile_lane % width == tile_row, 1.0, 0.0).astype(BF16)
    first = (((0,), (0,)), ((), ()))
    wide1 = lax.dot_general(p1_in[...], tiler, first, preferred_element_type=F32)
    wide2 = lax.dot_general(p2_in[...], tiler, first, preferred_element_type=F32)
    lane = lax.broadcasted_iota(jnp.int32, (feats, LANES), 1) // width
    for k in range(per):
        at = slice(k * feats, (k + 1) * feats)
        spread_proj[at, :LANES] = jnp.where(lane == k, wide1, 0.0).astype(BF16)
        spread_proj[at, LANES:] = jnp.where(lane == k, wide2, 0.0).astype(BF16)

    same = jnp.where(home == r, 1, 0)
    step = 8
    gain = gain_in[...]
    ones = jnp.ones((feats, feats), BF16)
    for k in range(parts):
        x_copy(k).wait()
        for n in range(seqs // step):
            block = x_in[n * step : (n + 1) * step, k * some : (k + 1) * some, :]
            wide = block.reshape(step * some, feats).astype(F32)
            rowsum = jnp.dot(block.reshape(step * some, feats), ones, preferred_element_type=F32)
            center = wide - rowsum * (1.0 / feats)
            square = center * center
            high = square.astype(BF16)
            rest = (square - high.astype(F32)).astype(BF16)
            spread = jnp.dot(high, ones, preferred_element_type=F32) + jnp.dot(
                rest, ones, preferred_element_type=F32
            )
            value = center * lax.rsqrt(spread * (1.0 / feats) + 1e-05) * gain
            for h in range(feats // LANES):
                normed[k, h, n * step * some : (n + 1) * step * some, :] = value[
                    :, h * LANES : (h + 1) * LANES
                ]
        for g in range(chunk):
            for j in range(per):
                for h in range(feats // LANES):
                    at = j * feats + h * LANES
                    stacked[k, g * seqs : (g + 1) * seqs, at : at + LANES] = normed[
                        k, h, pl.ds(per * g + j, seqs, stride=some), :
                    ].astype(BF16)
        both = jnp.dot(stacked[k], spread_proj[...], preferred_element_type=F32).astype(BF16)
        left_all[k, s] = both[:, :LANES].reshape(chunk, seqs, LANES)
        right_own[k] = both[:, LANES:].reshape(chunk, seqs, LANES)
        if k == 0:
            pl.semaphore_wait(barrier, n_seq - 1 + q * n_res - same)
        for d in range(2, n_seq, 2):
            left_copy(d, k, s).start()
        left_pass(0, k, s).start()
        right_start(k)

    for k in range(parts):
        for d in range(2, n_seq, 2):
            source = lax.rem(s + n_seq - d, n_seq)
            left_copy(d, k, source).wait_recv()
            left_pass(d, k, source).start()
    for k in range(parts):
        for d in range(0, n_seq, 2):
            left_copy(0, k, lax.rem(s + 1 - 2 * lax.rem(s, 2) + n_seq - d, n_seq)).wait_recv()
        for g in range(chunk):
            block = left_all[k, :, g].reshape(total, LANES).astype(F32).T
            for h in range(total // LANES):
                at = (k * chunk + g) * LANES
                left_t[h, at : at + LANES, :] = block[:, h * LANES : (h + 1) * LANES]
    for c in range(width):
        for h in range(total // LANES):
            left_mat[
                (c // 2) * rows : (c // 2 + 1) * rows,
                (c % 2) * total + h * LANES : (c % 2) * total + (h + 1) * LANES,
            ] = left_t[h, pl.ds(c, rows, stride=width), :].astype(BF16)
    for c in range(chunks):
        for t in range(n_seq):
            right_copy(0, 0, c, t).wait_recv()
    for k in range(parts):
        for d in range(2, n_seq, 2):
            left_copy(d, k, s).wait_send()
        for d in range(0, n_seq, 2):
            left_pass(d, k, s).wait_send()
    for k in range(parts):
        right_sent(k)


def pair_kernel(
    dims,
    left_hbm,
    right_hbm,
    w_hbm,
    off_hbm,
    out_ref,
    left_mat,
    right_all,
    w_ref,
    off_ref,
    right_mat,
    outer_mat,
    w_mat,
    out_buf,
    sem,
    in_sem,
):
    n_seq, n_res, seqs, rows, cols, width, cz, chunk = dims
    chunks = right_all.shape[0]
    total = n_seq * seqs
    half = LANES // 2
    some = cols // chunks
    arrive = [
        pltpu.make_async_copy(a, b, in_sem.at[n])
        for n, (a, b) in enumerate(
            [(w_hbm, w_ref), (left_hbm, left_mat), (right_hbm, right_all), (off_hbm, off_ref)]
        )
    ]
    for copy in arrive:
        copy.start()
    arrive[0].wait()

    def send(c):
        return pltpu.make_async_copy(
            out_buf.at[c].reshape(rows, some, cz),
            out_ref.at[:, c * some : (c + 1) * some],
            sem.at[c],
        )

    zero = jnp.zeros((width, cz), BF16)
    for c in range(width):
        part = w_ref[c * width : (c + 1) * width, :].astype(BF16)
        w_mat[2 * c * width : (2 * c + 1) * width, :cz] = part
        w_mat[2 * c * width : (2 * c + 1) * width, cz:] = zero
        w_mat[(2 * c + 1) * width : (2 * c + 2) * width, :cz] = zero
        w_mat[(2 * c + 1) * width : (2 * c + 2) * width, cz:] = part

    for copy in arrive[1:]:
        copy.wait()
    low = lax.broadcasted_iota(jnp.int32, (total, LANES), 1) < half
    scale = 1.0 / total
    for c in range(chunks):
        for g in range(chunk):
            block = right_all[c, :, g].reshape(total, LANES).astype(F32)
            turned = pltpu.roll(block, half, 1)
            right_mat[:total, :LANES] = jnp.where(low, block, 0.0).astype(BF16)
            right_mat[total:, :LANES] = jnp.where(low, 0.0, turned).astype(BF16)
            right_mat[:total, LANES:] = jnp.where(low, turned, 0.0).astype(BF16)
            right_mat[total:, LANES:] = jnp.where(low, 0.0, block).astype(BF16)
            outer = jnp.dot(left_mat[...], right_mat[...], preferred_element_type=F32).astype(BF16)
            for h in range(2):
                for p in range(width // 2):
                    outer_mat[
                        (2 * g + h) * rows : (2 * g + h + 1) * rows, p * LANES : (p + 1) * LANES
                    ] = outer[p * rows : (p + 1) * rows, h * LANES : (h + 1) * LANES]
        result = jnp.dot(outer_mat[...], w_mat[...], preferred_element_type=F32)
        for p in range(2 * chunk):
            for h in range(2):
                col = p * 2 + h
                out_buf[c, pl.ds(col, rows, stride=some), :] = (
                    result[p * rows : (p + 1) * rows, h * cz : (h + 1) * cz] * scale + off_ref[...]
                )
        send(c).start()
    for c in range(chunks):
        send(c).wait()


def local(n_seq, n_res, features, gain, p1, p2, w, offset):
    seqs, rows, feats = features.shape
    width = p1.shape[1]
    cz = w.shape[1]
    cols = rows * n_res // n_seq
    per = LANES // width
    blocks = rows // per
    q = n_seq // n_res
    own = blocks // q
    chunk = 4
    chunks = own // chunk
    total = n_seq * seqs
    dims = (n_seq, n_res, seqs, rows, cols, width, cz, chunk)
    parts = blocks // chunk
    hbm = pl.BlockSpec(memory_space=pltpu.HBM)
    vmem = pl.BlockSpec(memory_space=pltpu.VMEM)
    left, right = pl.pallas_call(
        functools.partial(kernel, dims),
        out_shape=[
            jax.ShapeDtypeStruct((width // 2 * rows, 2 * total), BF16),
            jax.ShapeDtypeStruct((chunks, n_seq, chunk, seqs, LANES), BF16),
        ],
        in_specs=[hbm] * 4,
        out_specs=[vmem] * 2,
        scratch_shapes=[
            pltpu.VMEM((seqs, rows, feats), BF16),
            pltpu.VMEM((1, feats), F32),
            pltpu.VMEM((width, feats), BF16),
            pltpu.VMEM((width, feats), BF16),
            pltpu.VMEM((parts, feats // LANES, seqs * per * chunk, LANES), F32),
            pltpu.VMEM((parts, chunk * seqs, per * feats), BF16),
            pltpu.VMEM((per * feats, 2 * LANES), BF16),
            pltpu.VMEM((parts, n_seq, chunk, seqs, LANES), BF16),
            pltpu.VMEM((parts, chunk, seqs, LANES), BF16),
            pltpu.VMEM((total // LANES, rows * width, LANES), F32),
            pltpu.SemaphoreType.DMA((n_seq, parts)),
            pltpu.SemaphoreType.DMA((n_seq, parts)),
            pltpu.SemaphoreType.DMA((n_seq, chunks)),
            pltpu.SemaphoreType.DMA((n_seq, chunks)),
            pltpu.SemaphoreType.DMA((parts,)),
            pltpu.SemaphoreType.DMA((3,)),
        ],
        compiler_params=pltpu.CompilerParams(
            collective_id=0, has_side_effects=True, vmem_limit_bytes=62 * 1024 * 1024
        ),
    )(features, gain.reshape(1, feats), p1.T, p2.T)
    return pl.pallas_call(
        functools.partial(pair_kernel, dims),
        out_shape=jax.ShapeDtypeStruct((rows, cols, cz), F32),
        in_specs=[hbm] * 4,
        out_specs=hbm,
        scratch_shapes=[
            pltpu.VMEM(left.shape, BF16),
            pltpu.VMEM(right.shape, BF16),
            pltpu.VMEM(w.shape, F32),
            pltpu.VMEM((1, cz), F32),
            pltpu.VMEM((2 * total, 2 * LANES), BF16),
            pltpu.VMEM((chunk * 2 * rows, width // 2 * LANES), BF16),
            pltpu.VMEM((2 * width * width, 2 * cz), BF16),
            pltpu.VMEM((chunks, rows * (cols // chunks), cz), F32),
            pltpu.SemaphoreType.DMA((chunks,)),
            pltpu.SemaphoreType.DMA((4,)),
        ],
        compiler_params=pltpu.CompilerParams(vmem_limit_bytes=62 * 1024 * 1024),
    )(left, right, w, offset.reshape(1, cz))


def solution(mesh):
    return jax.shard_map(
        functools.partial(local, mesh.shape["seq"], mesh.shape["res"]),
        mesh=mesh,
        in_specs=(P(("grp", "seq"), "res", None), P(), P(), P(), P(), P()),
        out_specs=P(("grp", "res"), "seq", None),
        check_vma=False,
    )
```
